128 devices in a mesh: seg: 16 (over x, z), sub: 8 (over y, core).
Axes of the slice: x: 4, y: 4, z: 4, core: 2. Of those that a mesh axis runs over, the one named last changes fastest.
Arguments:
- points: float32 [3, 524288], P(None, ('seg', 'sub')), may hold values from 0 to 1
- forces: float32 [3, 524288], P(None, ('seg', 'sub')), may hold values from -2 to 2
- near_leaf: int32 [4096, 13], P(('seg', 'sub')), may hold values from 0 to 31
- far_owner: int32 [4096, 14], P(('seg', 'sub')), may hold values from 0 to 127, all different within a row; in each aligned block of 32 rows (0 to 31, 32 to 63, ...) at most 7 rows name the same one
- far_slot: int32 [4096, 14], P(('seg', 'sub')), may hold values from 0 to 31
Outputs:
- potential: float32 [3, 524288], P(None, ('seg', 'sub'))
The draws below stay inside these ranges and needn't reach their ends.
Inputs may be any that keep to these rules, and one draw needn't show every extreme that they name: `far_owner`: the 14 owners named by one leaf differ. Among the leaves of one device (aligned blocks of 32 rows) no owner is named more than 7 times, a bound that some block reaches.
All inputs are finite; a program needn't handle non-finite values.
Results may differ from the reference program's by a relative error of at most 0.00002.
Values sent between devices are 32-bit elements; how exact they have to be, the bound alone decides.
No kernel may reach another device: no remote copies, remote signals or barrier semaphores. Data moves between devices by JAX's collectives and lax.ppermute only.
A program may use at most 128 MiB of HBM per device.

```python
import math
import jax
import jax.numpy as jnp
import numpy as np
from jax import lax

LEAF = 128
LEAF_DEV = 32
NEAR = 13
FAR = 14
CAP = 7
LEAVES = 4096
NPTS = 524288
DEVICES = 128


def with_ends(values, key, least, high):
    index_at = [jax.random.randint(jax.random.fold_in(key, axis), (), 0, length) for axis, length in enumerate(values.shape)]
    widest = values.shape.index(max(values.shape))
    beside = index_at[:widest] + [(index_at[widest] + 1) % values.shape[widest]] + index_at[widest + 1:]
    return values.at[tuple(index_at)].set(least).at[tuple(beside)].set(high)


def levels(stream_key, dims, cuts, least, largest):
    def one(position, blocks):
        draws = jax.random.uniform(jax.random.fold_in(jax.random.fold_in(stream_key, 6), position), (blocks,), jnp.float32, least / len(cuts), largest / len(cuts))
        return jnp.repeat(jnp.exp(draws), dims[position] // blocks).reshape((-1,) + (1,) * (len(dims) - position - 1))

    gain = one(*cuts[0])
    for cut in cuts[1:]:
        gain = gain * one(*cut)
    return gain


def deal_out(stream_key, own, number, rows, count, top, limit, skew):
    ranking = jax.random.permutation(stream_key, count)
    crowded, common = shares(count, rows * top, limit, skew, True), shares(count, rows * top, limit, skew, False)
    places = jnp.arange(count)

    def named(tallies, offset_by):
        used = int((tallies > 0).sum())
        fixed = max(1, used // 4)
        shifted = fixed + (places - fixed + offset_by * (used - fixed)) % max(1, count - fixed)
        return jnp.zeros((count,), jnp.int32).at[ranking[jnp.where(places < fixed, places, shifted)]].set(jnp.asarray(tallies, jnp.int32))

    tallies = jnp.where(number % 4 == 0, named(crowded, number // 4), named(common, number - number // 4 - 1))
    mixed = jax.random.permutation(jax.random.fold_in(own, 3), count)
    donor, receiver = mixed[0:count // 2 * 2:2], mixed[1:count // 2 * 2:2]
    margin = jnp.minimum(tallies[donor] - 1, limit - tallies[receiver]) // 2
    margin = jnp.where((donor == ranking[0]) | (receiver == ranking[0]) | (tallies[receiver] == 0), 0, jnp.maximum(margin, 0))
    shifted = jax.random.randint(jax.random.fold_in(own, 4), (count // 2,), 0, 1 << 20) % (margin + 1)
    tallies = tallies.at[donor].add(-shifted).at[receiver].add(shifted)
    items = jnp.searchsorted(jnp.cumsum(tallies), jnp.arange(rows * top), side="right").astype(jnp.int32)
    listing = items.reshape(top, rows).T
    listing = listing[jax.random.permutation(jax.random.fold_in(own, 1), rows)]
    offset_by = jax.random.randint(jax.random.fold_in(own, 2), (rows, 1), 0, top)
    return jnp.take_along_axis(listing, (jnp.arange(top)[None, :] + offset_by) % top, axis=1)


def shares(amount, total, bound, slope, full):
    weights = [(1 << 20) // math.isqrt(rank ** slope) + 1 for rank in range(1, amount + 1)]
    largest = bound if full else min(bound, max(-(-total // amount), total * weights[0] // sum(weights)))
    least = 1 if total - largest >= amount - 1 else 0
    counts, spare = [largest] + [least] * (amount - 1), total - largest - least * (amount - 1)
    while spare > 0:
        movable = [i for i in range(1, amount) if counts[i] < largest] or [i for i in range(1, amount) if counts[i] < bound]
        whole, budget = sum([weights[i] for i in movable]), spare
        for i in movable:
            extra = min(bound - counts[i], max(1, budget * weights[i] // whole), spare)
            counts[i] = counts[i] + extra
            spare = spare - extra
    return np.array(counts)


def gaussian(key, extent, width, limit, cuts=(), held_as=jnp.bfloat16):
    entries = jax.random.normal(key, extent, jnp.float32) * width
    if len(cuts) > 0:
        entries = levels(key, extent, cuts, -0.22, 0.18) * entries
    return jnp.clip(entries, min=-limit, max=limit).astype(held_as)


def setup_inputs(seed: int = 0) -> dict:
    arg_keys = jax.random.split(jax.random.key(seed), 6)
    points = jnp.clip(1.0 * jax.random.uniform(arg_keys[0], (3, NPTS), jnp.float32) ** levels(arg_keys[0], (3, NPTS), ((1, 128),), -0.2, 0.2), 0.0, 1.0)
    forces = gaussian(arg_keys[1], (3, NPTS), (8.0 / (LEAF * (NEAR + FAR)) ** 0.5), 2.0, ((1, 128),), jnp.float32)
    near_leaf = with_ends(jax.random.randint(arg_keys[2], (LEAVES, NEAR), 0, LEAF_DEV), jax.random.fold_in(arg_keys[2], 1), 0, LEAF_DEV - 1).astype(jnp.int32)
    far_owner_keys = jax.random.split(jax.random.fold_in(arg_keys[3], 1), LEAVES // LEAF_DEV)
    far_owner_turns = jax.random.permutation(jax.random.fold_in(arg_keys[3], 3), LEAVES // LEAF_DEV)
    far_owner = jax.vmap(lambda own, number: deal_out(jax.random.fold_in(arg_keys[3], 2), own, number, LEAF_DEV, DEVICES, FAR, CAP, 2))(far_owner_keys, far_owner_turns).reshape((LEAVES, FAR))
    far_slot = with_ends(jax.random.randint(arg_keys[4], (LEAVES, FAR), 0, LEAF_DEV), jax.random.fold_in(arg_keys[4], 1), 0, LEAF_DEV - 1).astype(jnp.int32)
    return dict(points=points, forces=forces, near_leaf=near_leaf, far_owner=far_owner, far_slot=far_slot)


shear_term = 1.0 / (4.0 * math.pi)
couple_term = shear_term / (4.0 * (1.0 - 0.3))
radius_soft = 0.05

def kelvinlet(targets, sources):
    offsets = targets[..., :, :, None] - sources[..., :3, None, :]
    squared = lax.optimization_barrier(jnp.sum(offsets * offsets, axis=-3))
    inverse = lax.rsqrt(squared + radius_soft * radius_soft)
    inverse_cube = inverse * inverse * inverse
    weight = (shear_term - couple_term) * inverse + 0.5 * shear_term * radius_soft * radius_soft * inverse_cube
    loads = sources[..., 3:, None, :]
    projected = lax.optimization_barrier(jnp.sum(offsets * loads, axis=-3))
    coupled = couple_term * inverse_cube * projected
    return lax.optimization_barrier(jnp.sum(weight[..., None, :, :] * loads + coupled[..., None, :, :] * offsets, axis=-1))

def reference(points, forces, near_leaf, far_owner, far_slot):
    leaves = points.shape[1] // LEAF
    blocks = jnp.concatenate([points.reshape(3, leaves, LEAF), forces.reshape(3, leaves, LEAF)], 0).transpose(1, 0, 2)
    first_leaf = jnp.arange(leaves, dtype=jnp.int32) // LEAF_DEV * LEAF_DEV
    near_global = near_leaf.astype(jnp.int32) + first_leaf[:, None]
    far_global = far_owner.astype(jnp.int32) * LEAF_DEV + far_slot.astype(jnp.int32)
    columns = jnp.concatenate([near_global, far_global], 1)

    def one_leaf(pieces):
        target, named = pieces
        sources = blocks[named]
        return lax.optimization_barrier(jnp.sum(kelvinlet(target[None], sources), axis=0))
    result = lax.map(one_leaf, (blocks[:, :3], columns))
    return result.transpose(1, 0, 2).reshape(3, leaves * LEAF)
```

```python
import functools
import math

import jax
import jax.numpy as jnp
from jax import lax
from jax.experimental import pallas as pl
from jax.experimental.pallas import tpu as pltpu
from jax.sharding import PartitionSpec as P

A = 1.0 / (4.0 * math.pi)
B = A / (4.0 * (1.0 - 0.3))
E = 0.05
C1 = A - B
C2 = A * E * E / 2
K2 = C1 / C2
WSC = C1 * math.sqrt(K2)
QK = B / C1 * K2
KE = K2 * E * E
CAP = 7
PER = 48
f32 = jnp.float32
bf16 = jnp.bfloat16
PA=['y0','y1','y2','f0','f1','f2','y0','y0','y0','y1','y1','y1','y2','y2','y2',None]
PB=[None]*6+['f0','f1','f2','f0','f1','f2','f0','f1','f2',None]
PC=[None,'f0','f1','f2']*2
PD=[None,'y0','y1','y2']*2
ROWS=PA+PB+PC+PD
NEED={n:[i for i,r in enumerate(ROWS) if r==n] for n in ('y0','y1','y2','f0','f1','f2')}
NAMES=('y0','y1','y2','f0','f1','f2')

def split3(v):
    a=v.astype(bf16); r=v-a.astype(f32)
    b=r.astype(bf16); r=r-b.astype(f32)
    return a,b,r.astype(bf16)

def lin_coef(table,row):
    co=[0.0]*3
    if table==0:
        if row<3: co[row]=-2.0*K2
        return co
    i=table-1
    if 6<=row<15:
        a,b=divmod(row-6,3)
        if i==b: co[a]-=2.0*K2
        if i==a: co[b]-=QK
        if a==b: co[i]-=QK
    return co

def const_rows(vals):
    r=lax.broadcasted_iota(jnp.int32,(8,128),0)
    v=jnp.full((8,128),vals[0],f32)
    for k in range(1,8): v=jnp.where(r==k,vals[k],v)
    return v

def kern(n_src, near, idx_ref, tgt_ref, *rest):
    if near:
        y_src,f_src,out_ref,w_ref,cen_ref,st_ref,co_ref,lhs_ref=rest
        def row(c,s):
            return y_src[c,pl.ds(s,1),:] if c<3 else f_src[c-3,pl.ds(s,1),:]
    else:
        src_ref,out_ref,w_ref,cen_ref,st_ref,co_ref,lhs_ref=rest
        def row(c,s): return src_ref[pl.ds(s+c,1),:]
    n=tgt_ref.shape[1]
    for g in range(0,n,8):
        for c in range(3):
            v=tgt_ref[c,g:g+8,:]
            cen_ref[c,g:g+8,:]=jnp.broadcast_to(jnp.mean(v,axis=1,keepdims=True),(8,128))
    for T in range(4):
        for H in range(2):
            for a in range(3):
                co_ref[(T*2+H)*3+a]=const_rows([lin_coef(T,8*H+r)[a] for r in range(8)])
    def init(l,_):
        st_ref[l]=jnp.ones((48,128),f32)
        if near:
            fill(l,l)
        return 0
    def fill(l,s):
        for c,nm in enumerate(NAMES):
            v=row(c,s)
            for i in NEED[nm]: st_ref[l,i:i+1,:]=v
    lax.fori_loop(0,st_ref.shape[0],init,0)
    sub=lax.broadcasted_iota(jnp.int32,(8,128),0)
    r16=lax.broadcasted_iota(jnp.int32,(16,512),0); l16=lax.broadcasted_iota(jnp.int32,(16,512),1)//128
    wone=jnp.where((r16<12)&(r16%4==l16),1.0,0.0).astype(bf16)
    for sl in range(2):
        w_ref[sl,96:112,:]=wone
        w_ref[sl,112:128,:]=jnp.zeros((16,512),bf16)
    def prep_w(t,slot):
        x=[jnp.broadcast_to(tgt_ref[c,pl.ds(t,1),:]-cen_ref[c,pl.ds(t,1),:],(8,128)) for c in range(3)]
        xx=K2*(x[0]*x[0]+x[1]*x[1]+x[2]*x[2])
        xj=QK*jnp.where(sub==3,x[0],jnp.where(sub==4,x[1],jnp.where(sub==5,x[2],0.0)))
        for T in range(4):
            hs=[]
            for H in range(2):
                v=None
                for a in range(3):
                    if any(lin_coef(T,8*H+r)[a]!=0 for r in range(8)):
                        w=co_ref[(T*2+H)*3+a]*x[a]
                        v=w if v is None else v+w
                if v is None: v=jnp.zeros((8,128),f32)
                if T==0 and H==1: v=jnp.where(sub==7,xx,v)
                if T>0 and H==0: v=v+x[T-1]*xj+jnp.where(sub==2+T,xx,0.0)
                hs.append(v)
            b1,b2,b3=split3(jnp.concatenate(hs,0))
            ls=slice(128*T,128*T+128)
            for blk,b in enumerate((b1,b2,b3,b1,b2,b1)):
                w_ref[slot,16*blk:16*blk+16,ls]=b
    def prep_leaf(t,k,slot,cenA,cenD,cen):
        s=idx_ref[t,k]
        if near: l=s
        else:
            l=k; fill(l,s)
        y=[jnp.broadcast_to(row(c,s),(8,128))-cen[c] for c in range(3)]
        f=[jnp.broadcast_to(row(3+c,s),(8,128)) for c in range(3)]
        Y=K2*(y[0]*y[0]+y[1]*y[1]+y[2]*y[2])+jnp.where(sub%4==0,KE,KE+1.0)
        yf=QK*(y[0]*f[0]+y[1]*f[1]+y[2]*f[2])
        t48=st_ref[l]
        V=(t48[0:16]-cenA)*t48[16:32]
        C=t48[32:40]*Y+yf*(t48[40:48]-cenD)
        C=jnp.where(sub%4==0,Y,C)
        a,b,c=split3(V)
        p=C.astype(bf16).astype(f32); r=C-p
        o=r.astype(bf16).astype(f32); r=r-o
        cc=jnp.concatenate([jnp.where(sub<4,p,o),jnp.where(sub<4,r,0.0)],0).astype(bf16)
        at=jnp.concatenate([a,a,a,b,b,c,cc,cc],0)
        lhs_ref[slot,128*k:128*k+128,:]=jnp.transpose(at)
    def cens(t):
        cen=[jnp.broadcast_to(cen_ref[c,pl.ds(t,1),:],(8,128)) for c in range(3)]
        def pat(rows):
            v=jnp.zeros((8,128),f32)
            for c in range(3):
                for k,nm in enumerate(rows):
                    if nm=='y%d'%c: v=jnp.where(sub==k,cen[c],v)
            return v
        return jnp.concatenate([pat(PA[:8]),pat(PA[8:])],0),pat(PD),cen
    def prep_all(t,slot):
        prep_w(t,slot)
        cs=cens(t)
        for k in range(n_src): prep_leaf(t,k,slot,*cs)
    def step(t,slot):
        tn=jnp.minimum(t+1,n-1); ns=1-slot
        T=lax.dot_general(lhs_ref[slot],w_ref[slot],(((1,),(0,)),((),())),preferred_element_type=f32)
        cs=cens(tn)
        acc=[jnp.zeros((8,128),f32) for _ in range(3)]
        prep_w(tn,ns)
        for k in range(n_src):
            for rr in range(16*k,16*k+16):
                S=T[8*rr:8*rr+8,0:128]
                h=lax.rsqrt(S); e=h*h*h
                acc=[acc[c]+e*T[8*rr:8*rr+8,128*(c+1):128*(c+2)] for c in range(3)]
            prep_leaf(tn,k,ns,*cs)
        for c in range(3):
            out_ref[c,pl.ds(t,1),:]=jnp.sum(acc[c],axis=0,keepdims=True)*WSC
    prep_all(0,0)
    def body(i,_):
        step(2*i,0); step(2*i+1,1)
        return 0
    lax.fori_loop(0,n//2,body,0)

def call(n_src, near, idx, tgt, *src):
    n=tgt.shape[1]
    vm=pl.BlockSpec(memory_space=pltpu.VMEM)
    return pl.pallas_call(functools.partial(kern,n_src,near), out_shape=jax.ShapeDtypeStruct((3,n,128),f32),
            in_specs=[pl.BlockSpec(memory_space=pltpu.SMEM)]+[vm]*(1+len(src)),
            out_specs=vm,
            scratch_shapes=[pltpu.VMEM((2,128,512),bf16),pltpu.VMEM((3,n,128),f32),pltpu.VMEM((n if near else n_src,48,128),f32),
              pltpu.VMEM((24,8,128),f32),pltpu.VMEM((2,n_src*128,128),bf16)],
            name="near" if near else "far",
            cost_estimate=pl.CostEstimate(flops=20000000000,bytes_accessed=1000000,transcendentals=0),
            compiler_params=pltpu.CompilerParams(vmem_limit_bytes=40<<20))(idx,tgt,*src)


def request_kernel(owner_ref, slot_ref, want_ref, base_ref):
    rows, far = owner_ref.shape
    lane = lax.broadcasted_iota(jnp.int32, (rows, 128), 1)
    named = jnp.zeros((rows, 128), f32)
    slots = jnp.zeros((rows, 128), f32)
    hits = []
    for k in range(far):
        hit = jnp.where(owner_ref[:, k:k+1] == lane, 1.0, 0.0)
        hits.append(hit)
        named = named + hit
        slots = slots + hit * slot_ref[:, k:k+1].astype(f32)
    before = lax.broadcasted_iota(jnp.int32, (rows, rows), 1) < lax.broadcasted_iota(jnp.int32, (rows, rows), 0)
    rank = jnp.dot(before.astype(bf16), named.astype(bf16), preferred_element_type=f32)
    wanted = [jnp.sum(jnp.where(rank == r, slots, 0.0), axis=0, keepdims=True) for r in range(CAP)]
    wanted = jnp.concatenate(wanted + [jnp.zeros((128 - CAP, 128), f32)], 0)
    want_ref[...] = jnp.transpose(wanted).astype(jnp.int32)
    base = jnp.zeros((rows, 128), jnp.int32)
    for k in range(far):
        mine = jnp.sum(hits[k] * rank, axis=1, keepdims=True).astype(jnp.int32) * 6 + owner_ref[:, k:k+1] * PER
        base = jnp.where(lane == k, mine, base)
    base_ref[...] = base[:, :far]


def reply_kernel(ask_ref, y_ref, f_ref, out_ref):
    def one(p, _):
        for r in range(CAP):
            s = ask_ref[p, r]
            for c in range(6):
                v = y_ref[c, pl.ds(s, 1), :] if c < 3 else f_ref[c - 3, pl.ds(s, 1), :]
                out_ref[pl.ds(p * PER + 6 * r + c, 1), :] = v
        return 0
    lax.fori_loop(0, ask_ref.shape[0], one, 0)


def per_device(points, forces, near_leaf, far_owner, far_slot):
    n = near_leaf.shape[0]
    devices = lax.axis_size(("seg", "sub"))
    y = points.reshape(3, n, 128)
    f = forces.reshape(3, n, 128)
    vm = pl.BlockSpec(memory_space=pltpu.VMEM)
    sm = pl.BlockSpec(memory_space=pltpu.SMEM)
    want, base = pl.pallas_call(
        request_kernel,
        out_shape=(jax.ShapeDtypeStruct((devices, 128), jnp.int32), jax.ShapeDtypeStruct(far_owner.shape, jnp.int32)),
        in_specs=[vm, vm], out_specs=(vm, vm), name="requests",
    )(far_owner, far_slot)
    asked = lax.all_to_all(want.reshape(devices, 1, 128), ("seg", "sub"), split_axis=0, concat_axis=0, tiled=True)
    reply = pl.pallas_call(
        reply_kernel,
        out_shape=jax.ShapeDtypeStruct((devices * PER, 128), f32),
        in_specs=[sm, vm, vm], out_specs=vm, name="replies",
        compiler_params=pltpu.CompilerParams(vmem_limit_bytes=32 << 20),
    )(asked.reshape(devices, 128), y, f)
    answers = lax.all_to_all(reply.reshape(devices, PER, 128), ("seg", "sub"), split_axis=0, concat_axis=0, tiled=True)
    near = call(near_leaf.shape[1], True, near_leaf, y, y, f)
    far = call(far_owner.shape[1], False, base, y, answers.reshape(devices * PER, 128))
    return (near + far).reshape(3, n * 128)


def solution(mesh):
    split = P(None, ("seg", "sub"))
    rows = P(("seg", "sub"), None)
    return jax.shard_map(
        per_device, mesh=mesh, in_specs=(split, split, rows, rows, rows), out_specs=split, check_vma=False
    )
```

```python
import functools
import math

import jax
import jax.numpy as jnp
from jax import lax
from jax.experimental import pallas as pl
from jax.experimental.pallas import tpu as pltpu
from jax.sharding import PartitionSpec as P

A = 1.0 / (4.0 * math.pi)
B = A / (4.0 * (1.0 - 0.3))
E = 0.05
C1 = A - B
C2 = A * E * E / 2
K2 = C1 / C2
WSC = C1 * math.sqrt(K2)
QK = B / C1 * K2
KE = K2 * E * E
CAP = 56
FIRST = 28
PER_A = 6 * FIRST
PER_B = 6 * (CAP - FIRST)
UNIT = 7
f32 = jnp.float32
bf16 = jnp.bfloat16
PA=['y0','y1','y2','f0','f1','f2','y0','y0','y0','y1','y1','y1','y2','y2','y2',None]
PB=[None]*6+['f0','f1','f2','f0','f1','f2','f0','f1','f2',None]
PC=[None,'f0','f1','f2']*2
PD=[None,'y0','y1','y2']*2
ROWS=PA+PB+PC+PD
NEED={n:[i for i,r in enumerate(ROWS) if r==n] for n in ('y0','y1','y2','f0','f1','f2')}
NAMES=('y0','y1','y2','f0','f1','f2')

def split3(v):
    a=v.astype(bf16); r=v-a.astype(f32)
    b=r.astype(bf16); r=r-b.astype(f32)
    return a,b,r.astype(bf16)

def lin_coef(table,row):
    co=[0.0]*3
    if table==0:
        if row<3: co[row]=-2.0*K2
        return co
    i=table-1
    if 6<=row<15:
        a,b=divmod(row-6,3)
        if i==b: co[a]-=2.0*K2
        if i==a: co[b]-=QK
        if a==b: co[i]-=QK
    return co

def const_rows(vals):
    r=lax.broadcasted_iota(jnp.int32,(8,128),0)
    v=jnp.full((8,128),vals[0],f32)
    for k in range(1,8): v=jnp.where(r==k,vals[k],v)
    return v

def pair_kernel(mode, n_src, *refs):
    near = mode == "near"
    w_ref, cen_ref, st_ref, co_ref, lhs_ref, order_ref = refs[-6:]
    out_ref = refs[-7]
    if near:
        idx_ref, _, y_ref, f_ref = refs[:4]
    elif mode == "first":
        idx_ref, top_ref, y_ref, part_ref, a_ref = refs[:5]
    else:
        idx_ref, top_ref, y_ref, part_ref, a_ref, b_ref = refs[:6]
    n = y_ref.shape[1] // 128

    def lanes(s):
        return pl.ds(pl.multiple_of(s * 128, 128), 128)

    def fetch(s):
        if near:
            return [y_ref[c:c+1, lanes(s)] for c in range(3)] + [f_ref[c:c+1, lanes(s)] for c in range(3)]
        last = a_ref.shape[0] - 6
        if mode == "first":
            s = jnp.minimum(s, last)
            return [a_ref[pl.ds(s + c, 1), :] for c in range(6)]
        late = s > last
        sa = jnp.where(late, 0, s)
        sb = jnp.where(late, s - a_ref.shape[0], 0)
        return [jnp.where(late, b_ref[pl.ds(sb + c, 1), :], a_ref[pl.ds(sa + c, 1), :]) for c in range(6)]

    for t in range(n):
        v = y_ref[:, 128*t:128*t+128]
        cen_ref[t, 0:3, :] = jnp.broadcast_to(jnp.mean(v, axis=1, keepdims=True), (3, 128))
    for T in range(4):
        for H in range(2):
            for a in range(3):
                co_ref[(T*2+H)*3+a] = const_rows([lin_coef(T, 8*H+r)[a] for r in range(8)])

    def fill(l, rows):
        for c, nm in enumerate(NAMES):
            for i in NEED[nm]:
                st_ref[l, i:i+1, :] = rows[c]

    def init(l, _):
        st_ref[l] = jnp.ones((48, 128), f32)
        if near:
            fill(l, fetch(l))
        return 0
    lax.fori_loop(0, st_ref.shape[0], init, 0)

    sub = lax.broadcasted_iota(jnp.int32, (8, 128), 0)
    r16 = lax.broadcasted_iota(jnp.int32, (16, 512), 0)
    l16 = lax.broadcasted_iota(jnp.int32, (16, 512), 1) // 128
    wone = jnp.where((r16 < 12) & (r16 % 4 == l16), 1.0, 0.0).astype(bf16)
    for sl in range(2):
        w_ref[sl, 96:112, :] = wone
        w_ref[sl, 112:128, :] = jnp.zeros((16, 512), bf16)

    if near:
        count = n
    else:
        out_ref[...] = part_ref[...]

        def sort(u, count):
            ready = top_ref[u % 2, u // 2] < FIRST
            order_ref[count] = u
            return count + jnp.where(ready == (mode == "first"), 1, 0)
        count = lax.fori_loop(0, 2 * n, sort, 0)

    def place(i):
        if near:
            t = jnp.minimum(i, n - 1)
            return t, lambda k: idx_ref[k, t]
        u = order_ref[jnp.maximum(jnp.minimum(i, count - 1), 0)]
        t = u // 2
        return t, lambda k: idx_ref[(u % 2) * UNIT + k, t]

    def prep_w(t, slot):
        x = [jnp.broadcast_to(y_ref[c:c+1, lanes(t)] - cen_ref[t, c:c+1, :], (8, 128)) for c in range(3)]
        xx = K2*(x[0]*x[0]+x[1]*x[1]+x[2]*x[2])
        xj = QK*jnp.where(sub == 3, x[0], jnp.where(sub == 4, x[1], jnp.where(sub == 5, x[2], 0.0)))
        for T in range(4):
            hs = []
            for H in range(2):
                v = None
                for a in range(3):
                    if any(lin_coef(T, 8*H+r)[a] != 0 for r in range(8)):
                        w = co_ref[(T*2+H)*3+a]*x[a]
                        v = w if v is None else v+w
                if v is None:
                    v = jnp.zeros((8, 128), f32)
                if T == 0 and H == 1:
                    v = jnp.where(sub == 7, xx, v)
                if T > 0 and H == 0:
                    v = v+x[T-1]*xj+jnp.where(sub == 2+T, xx, 0.0)
                hs.append(v)
            b1, b2, b3 = split3(jnp.concatenate(hs, 0))
            ls = slice(128*T, 128*T+128)
            for blk, b in enumerate((b1, b2, b3, b1, b2, b1)):
                w_ref[slot, 16*blk:16*blk+16, ls] = b

    def prep_leaf(s, k, slot, cenA, cenD, cen):
        rows = fetch(s)
        if near:
            l = s
        else:
            l = k
            fill(l, rows)
        y = [jnp.broadcast_to(rows[c], (8, 128))-cen[c] for c in range(3)]
        f = [jnp.broadcast_to(rows[3+c], (8, 128)) for c in range(3)]
        Y = K2*(y[0]*y[0]+y[1]*y[1]+y[2]*y[2])+jnp.where(sub % 4 == 0, KE, KE+1.0)
        yf = QK*(y[0]*f[0]+y[1]*f[1]+y[2]*f[2])
        t48 = st_ref[l]
        V = (t48[0:16]-cenA)*t48[16:32]
        C = t48[32:40]*Y+yf*(t48[40:48]-cenD)
        C = jnp.where(sub % 4 == 0, Y, C)
        a, b, c = split3(V)
        p = C.astype(bf16).astype(f32)
        r = C-p
        o = r.astype(bf16).astype(f32)
        r = r-o
        cc = jnp.concatenate([jnp.where(sub < 4, p, o), jnp.where(sub < 4, r, 0.0)], 0).astype(bf16)
        at = jnp.concatenate([a, a, a, b, b, c, cc, cc], 0)
        lhs_ref[slot, 128*k:128*k+128, :] = jnp.transpose(at)

    def cens(t):
        cen = [jnp.broadcast_to(cen_ref[t, c:c+1, :], (8, 128)) for c in range(3)]

        def pat(rows):
            v = jnp.zeros((8, 128), f32)
            for c in range(3):
                for k, nm in enumerate(rows):
                    if nm == "y%d" % c:
                        v = jnp.where(sub == k, cen[c], v)
            return v
        return jnp.concatenate([pat(PA[:8]), pat(PA[8:])], 0), pat(PD), cen

    def prep_all(i, slot):
        t, src = place(i)
        prep_w(t, slot)
        cs = cens(t)
        for k in range(n_src):
            prep_leaf(src(k), k, slot, *cs)

    def step(i, slot):
        t, _ = place(i)
        tn, src = place(i + 1)
        ns = 1-slot
        T = lax.dot_general(lhs_ref[slot], w_ref[slot], (((1,), (0,)), ((), ())), preferred_element_type=f32)
        cs = cens(tn)
        acc = [jnp.zeros((8, 128), f32) for _ in range(3)]
        prep_w(tn, ns)
        for k in range(n_src):
            for rr in range(16*k, 16*k+16):
                S = T[8*rr:8*rr+8, 0:128]
                h = lax.rsqrt(S)
                e = h*h*h
                acc = [acc[c]+e*T[8*rr:8*rr+8, 128*(c+1):128*(c+2)] for c in range(3)]
            prep_leaf(src(k), k, ns, *cs)
        for c in range(3):
            total = jnp.sum(acc[c], axis=0, keepdims=True)*WSC
            if near:
                out_ref[c:c+1, lanes(t)] = total
            else:
                out_ref[c:c+1, lanes(t)] += jnp.where(i < count, total, 0.0)

    prep_all(0, 0)

    def body(i, _):
        for j in range(4):
            step(4*i+j, j % 2)
        return 0
    lax.fori_loop(0, (count + 3)//4, body, 0)


VM = pl.BlockSpec(memory_space=pltpu.VMEM)
SM = pl.BlockSpec(memory_space=pltpu.SMEM)


def pairs(mode, n_src, scalars, arrays):
    n = arrays[0].shape[1] // 128
    return pl.pallas_call(
        functools.partial(pair_kernel, mode, n_src),
        out_shape=jax.ShapeDtypeStruct((3, n*128), f32),
        in_specs=[SM]*len(scalars)+[VM]*len(arrays), out_specs=VM,
        scratch_shapes=[
            pltpu.VMEM((2, 128, 512), bf16), pltpu.VMEM((n, 8, 128), f32),
            pltpu.VMEM((n if mode == "near" else n_src, 48, 128), f32), pltpu.VMEM((24, 8, 128), f32),
            pltpu.VMEM((2, n_src*128, 128), bf16), pltpu.SMEM((2*n+1,), jnp.int32)],
        name=mode, cost_estimate=pl.CostEstimate(flops=COST[mode], bytes_accessed=1000000, transcendentals=0),
        compiler_params=pltpu.CompilerParams(vmem_limit_bytes=40 << 20),
    )(*scalars, *arrays)


COST = {"near": 20000000000, "first": 16000000000, "rest": 6000000000}


def request_kernel(owner_ref, slot_ref, want_ref, base_ref, top_ref):
    far, rows = owner_ref.shape
    groups = want_ref.shape[0]
    my_y, my_core = lax.axis_index("y"), lax.axis_index("core")
    group = lax.broadcasted_iota(jnp.int32, (groups, rows), 0)
    hits = [jnp.where(lax.shift_right_logical(owner_ref[k:k+1, :], 3) == group, 1.0, 0.0) for k in range(far)]
    named = hits[0]
    for k in range(1, far):
        named = named + hits[k]
    before = lax.broadcasted_iota(jnp.int32, (rows, rows), 0) < lax.broadcasted_iota(jnp.int32, (rows, rows), 1)
    rank = jnp.dot(named.astype(bf16), before.astype(f32).astype(bf16), preferred_element_type=f32)
    place = lax.broadcasted_iota(jnp.int32, (128, rows), 0)
    want = jnp.zeros((groups, 128), f32)
    mine = []
    for k in range(far):
        own = jnp.sum(hits[k]*rank, axis=0, keepdims=True).astype(jnp.int32)
        rank = rank + hits[k]
        mine.append(own)
        o = owner_ref[k:k+1, :]
        dy = (lax.shift_right_logical(o, 1) - my_y) & 3
        dc = (o - my_core) & 1
        value = (dy*64 + dc*32 + slot_ref[k:k+1, :]).astype(f32)
        at = jnp.where(place == own, value, 0.0)
        want = want + lax.dot_general(hits[k].astype(bf16), at.astype(bf16), (((1,), (1,)), ((), ())),
                                      preferred_element_type=f32)
    want_ref[...] = want.astype(jnp.int32)
    base = []
    for k in range(far):
        asked = lax.shift_right_logical(owner_ref[k:k+1, :], 3)
        late = groups*PER_A + asked*PER_B + (mine[k]-FIRST)*6
        base.append(jnp.where(mine[k] >= FIRST, late, asked*PER_A + mine[k]*6))
    order = []
    for k in range(far):
        p = jnp.zeros((1, rows), jnp.int32)
        for j in range(far):
            if j != k:
                p = p + jnp.where((mine[j] < mine[k]) if j > k else (mine[j] <= mine[k]), 1, 0)
        order.append(p)
    for p in range(far):
        b = jnp.zeros((1, rows), jnp.int32)
        m = jnp.zeros((1, rows), jnp.int32)
        for k in range(far):
            b = b + jnp.where(order[k] == p, base[k], 0)
            if p % UNIT == UNIT-1:
                m = m + jnp.where(order[k] == p, mine[k], 0)
        base_ref[p:p+1, :] = b
        if p % UNIT == UNIT-1:
            top_ref[p//UNIT:p//UNIT+1, :] = m


def pack_kernel(y_ref, f_ref, after_ref, out_ref):
    for t in range(y_ref.shape[1] // 128):
        out_ref[8*t:8*t+3, :] = y_ref[:, 128*t:128*t+128]
        out_ref[8*t+3:8*t+6, :] = f_ref[:, 128*t:128*t+128]
        out_ref[8*t+6:8*t+8, :] = jnp.zeros((2, 128), f32)


def reply_kernel(ranks, *refs):
    ask_ref, *tables = refs[:5]
    out_ref, table_ref = refs[-2:]
    rows = tables[0].shape[0]
    for i, ref in enumerate(tables):
        table_ref[rows*i:rows*i+rows, :] = ref[...]

    def one(p, _):
        for q, r in enumerate(ranks):
            tile = table_ref[pl.ds(pl.multiple_of(ask_ref[p, r] * 8, 8), 8), :]
            out_ref[p, 6*q:6*q+6, :] = tile[0:6]
        return 0
    lax.fori_loop(0, out_ref.shape[0], one, 0)


def per_device(points, forces, near_leaf, far_owner, far_slot):
    n, near_count = near_leaf.shape
    far_count = far_owner.shape[1]
    groups = lax.axis_size("seg")
    i32 = jnp.int32
    want, base, top = pl.pallas_call(
        request_kernel,
        out_shape=(jax.ShapeDtypeStruct((groups, 128), i32), jax.ShapeDtypeStruct((far_count, n), i32),
                   jax.ShapeDtypeStruct((far_count//UNIT, n), i32)),
        in_specs=[VM, VM], out_specs=(VM, VM, VM), name="requests",
    )(far_owner.T, far_slot.T)

    def send(values):
        return lax.all_to_all(values, "seg", split_axis=0, concat_axis=0, tiled=True)
    asked = send(want.reshape(groups, 1, 128)).reshape(groups, 128)

    own = pl.pallas_call(
        pack_kernel, out_shape=jax.ShapeDtypeStruct((8*n, 128), f32), in_specs=[VM, VM, VM], out_specs=VM, name="pack",
    )(points, forces, want)
    chip = jnp.concatenate([own, lax.ppermute(own, "core", [(0, 1), (1, 0)])], 0)
    tables = [chip] + [lax.ppermute(chip, "y", [(i, (i - d) % 4) for i in range(4)]) for d in (1, 2, 3)]

    def answer(ranks, *after):
        reply = pl.pallas_call(
            functools.partial(reply_kernel, ranks),
            out_shape=jax.ShapeDtypeStruct((groups, 6*len(ranks), 128), f32),
            in_specs=[SM] + [VM]*(4 + len(after)), out_specs=VM,
            scratch_shapes=[pltpu.VMEM((64*n, 128), f32)], name="replies",
            compiler_params=pltpu.CompilerParams(vmem_limit_bytes=32 << 20),
        )(asked, *tables, *after)
        return reply, send(reply).reshape(-1, 128)
    reply_a, answers_a = answer(range(0, FIRST))
    near = pairs("near", near_count, (near_leaf.T, asked), (points, forces))
    reply_b, answers_b = answer(range(FIRST, CAP), near)
    first = pairs("first", UNIT, (base, top), (points, near, answers_a))
    return pairs("rest", UNIT, (base, top), (points, first, answers_a, answers_b))


def solution(mesh):
    grid = jax.sharding.Mesh(mesh.devices.reshape(mesh.devices.shape[0], -1, 2), ("seg", "y", "core"))
    every = ("seg", "y", "core")
    split = P(None, every)
    rows = P(every, None)
    return jax.shard_map(
        per_device, mesh=grid, in_specs=(split, split, rows, rows, rows), out_specs=split, check_vma=False
    )
```

```python
import functools
import math

import jax
import jax.numpy as jnp
from jax import lax
from jax.experimental import pallas as pl
from jax.experimental.pallas import tpu as pltpu
from jax.sharding import PartitionSpec as P

A = 1.0 / (4.0 * math.pi)
B = A / (4.0 * (1.0 - 0.3))
E = 0.05
C1 = A - B
C2 = A * E * E / 2
K2 = C1 / C2
WSC = C1 * math.sqrt(K2)
QK = B / C1 * K2
KE = K2 * E * E
CAP = 56
FIRST = 28
PER_A = 6 * FIRST
PER_B = 6 * (CAP - FIRST)
UNIT = 7
f32 = jnp.float32
bf16 = jnp.bfloat16
PA=['y0','y1','y2','f0','f1','f2','y0','y0','y0','y1','y1','y1','y2','y2','y2',None]
PB=[None]*6+['f0','f1','f2','f0','f1','f2','f0','f1','f2',None]
PC=[None,'f0','f1','f2']*2
PD=[None,'y0','y1','y2']*2
ROWS=PA+PB+PC+PD
NEED={n:[i for i,r in enumerate(ROWS) if r==n] for n in ('y0','y1','y2','f0','f1','f2')}
NAMES=('y0','y1','y2','f0','f1','f2')

def split3(v):
    a=v.astype(bf16); r=v-a.astype(f32)
    b=r.astype(bf16); r=r-b.astype(f32)
    return a,b,r.astype(bf16)

def lin_coef(table,row):
    co=[0.0]*3
    if table==0:
        if row<3: co[row]=-2.0*K2
        return co
    i=table-1
    if 6<=row<15:
        a,b=divmod(row-6,3)
        if i==b: co[a]-=2.0*K2
        if i==a: co[b]-=QK
        if a==b: co[i]-=QK
    return co

def const_rows(vals):
    r=lax.broadcasted_iota(jnp.int32,(8,128),0)
    v=jnp.full((8,128),vals[0],f32)
    for k in range(1,8): v=jnp.where(r==k,vals[k],v)
    return v

def pair_kernel(mode, n_src, *refs):
    near = mode == "near"
    w_ref, cen_ref, st_ref, co_ref, lhs_ref = refs[-5:]
    out_ref = refs[-6]
    if near:
        idx_ref, _, y_ref, f_ref = refs[:4]
    elif mode == "first":
        idx_ref, y_ref, part_ref, a_ref = refs[:4]
    else:
        idx_ref, y_ref, part_ref, a_ref, b_ref = refs[:5]
    n = y_ref.shape[1] // 128

    def lanes(s):
        return pl.ds(pl.multiple_of(s * 128, 128), 128)

    def fetch(s):
        if near:
            return [y_ref[c:c+1, lanes(s)] for c in range(3)] + [f_ref[c:c+1, lanes(s)] for c in range(3)]
        last = a_ref.shape[0] - 6
        if mode == "first":
            s = jnp.minimum(s, last)
            return [a_ref[pl.ds(s + c, 1), :] for c in range(6)]
        late = s > last
        sa = jnp.where(late, 0, s)
        sb = jnp.where(late, s - a_ref.shape[0], 0)
        return [jnp.where(late, b_ref[pl.ds(sb + c, 1), :], a_ref[pl.ds(sa + c, 1), :]) for c in range(6)]

    for t in range(n):
        v = y_ref[:, 128*t:128*t+128]
        cen_ref[t, 0:3, :] = jnp.broadcast_to(jnp.mean(v, axis=1, keepdims=True), (3, 128))
    for T in range(4):
        for H in range(2):
            for a in range(3):
                co_ref[(T*2+H)*3+a] = const_rows([lin_coef(T, 8*H+r)[a] for r in range(8)])

    def fill(l, rows):
        for c, nm in enumerate(NAMES):
            for i in NEED[nm]:
                st_ref[l, i:i+1, :] = rows[c]

    def init(l, _):
        st_ref[l] = jnp.ones((48, 128), f32)
        if near:
            fill(l, fetch(l))
        return 0
    lax.fori_loop(0, st_ref.shape[0], init, 0)

    sub = lax.broadcasted_iota(jnp.int32, (8, 128), 0)
    r16 = lax.broadcasted_iota(jnp.int32, (16, 512), 0)
    l16 = lax.broadcasted_iota(jnp.int32, (16, 512), 1) // 128
    wone = jnp.where((r16 < 12) & (r16 % 4 == l16), 1.0, 0.0).astype(bf16)
    for sl in range(2):
        w_ref[sl, 96:112, :] = wone
        w_ref[sl, 112:128, :] = jnp.zeros((16, 512), bf16)

    if near:
        count = n
    else:
        out_ref[...] = part_ref[...]

        units = 2*UNIT
        ready = idx_ref[units + 1, 0]
        first_unit = 0 if mode == "first" else ready
        count = ready if mode == "first" else 2*n - ready

    def place(i):
        if near:
            t = jnp.minimum(i, n - 1)
            return t, lambda k: idx_ref[k, t]
        u = idx_ref[units, first_unit + jnp.maximum(jnp.minimum(i, count - 1), 0)]
        t = u & 31
        half = lax.shift_right_logical(u, 5) * UNIT
        return t, lambda k: idx_ref[half + k, t]

    def prep_w(t, slot):
        x = [jnp.broadcast_to(y_ref[c:c+1, lanes(t)] - cen_ref[t, c:c+1, :], (8, 128)) for c in range(3)]
        xx = K2*(x[0]*x[0]+x[1]*x[1]+x[2]*x[2])
        xj = QK*jnp.where(sub == 3, x[0], jnp.where(sub == 4, x[1], jnp.where(sub == 5, x[2], 0.0)))
        for T in range(4):
            hs = []
            for H in range(2):
                v = None
                for a in range(3):
                    if any(lin_coef(T, 8*H+r)[a] != 0 for r in range(8)):
                        w = co_ref[(T*2+H)*3+a]*x[a]
                        v = w if v is None else v+w
                if v is None:
                    v = jnp.zeros((8, 128), f32)
                if T == 0 and H == 1:
                    v = jnp.where(sub == 7, xx, v)
                if T > 0 and H == 0:
                    v = v+x[T-1]*xj+jnp.where(sub == 2+T, xx, 0.0)
                hs.append(v)
            b1, b2, b3 = split3(jnp.concatenate(hs, 0))
            ls = slice(128*T, 128*T+128)
            for blk, b in enumerate((b1, b2, b3, b1, b2, b1)):
                w_ref[slot, 16*blk:16*blk+16, ls] = b

    def prep_leaf(s, k, slot, cenA, cenD, cen):
        rows = fetch(s)
        if near:
            l = s
        else:
            l = k
            fill(l, rows)
        y = [jnp.broadcast_to(rows[c], (8, 128))-cen[c] for c in range(3)]
        f = [jnp.broadcast_to(rows[3+c], (8, 128)) for c in range(3)]
        Y = K2*(y[0]*y[0]+y[1]*y[1]+y[2]*y[2])+jnp.where(sub % 4 == 0, KE, KE+1.0)
        yf = QK*(y[0]*f[0]+y[1]*f[1]+y[2]*f[2])
        t48 = st_ref[l]
        V = (t48[0:16]-cenA)*t48[16:32]
        C = t48[32:40]*Y+yf*(t48[40:48]-cenD)
        C = jnp.where(sub % 4 == 0, Y, C)
        a, b, c = split3(V)
        p = C.astype(bf16).astype(f32)
        r = C-p
        o = r.astype(bf16).astype(f32)
        r = r-o
        cc = jnp.concatenate([jnp.where(sub < 4, p, o), jnp.where(sub < 4, r, 0.0)], 0).astype(bf16)
        at = jnp.concatenate([a, a, a, b, b, c, cc, cc], 0)
        lhs_ref[slot, 128*k:128*k+128, :] = jnp.transpose(at)

    def cens(t):
        cen = [jnp.broadcast_to(cen_ref[t, c:c+1, :], (8, 128)) for c in range(3)]

        def pat(rows):
            v = jnp.zeros((8, 128), f32)
            for c in range(3):
                for k, nm in enumerate(rows):
                    if nm == "y%d" % c:
                        v = jnp.where(sub == k, cen[c], v)
            return v
        return jnp.concatenate([pat(PA[:8]), pat(PA[8:])], 0), pat(PD), cen

    def prep_all(i, slot):
        t, src = place(i)
        prep_w(t, slot)
        cs = cens(t)
        for k in range(n_src):
            prep_leaf(src(k), k, slot, *cs)

    def step(i, slot):
        t, _ = place(i)
        tn, src = place(i + 1)
        ns = 1-slot
        T = lax.dot_general(lhs_ref[slot], w_ref[slot], (((1,), (0,)), ((), ())), preferred_element_type=f32)
        cs = cens(tn)
        acc = [jnp.zeros((8, 128), f32) for _ in range(3)]
        prep_w(tn, ns)
        for k in range(n_src):
            for rr in range(16*k, 16*k+16):
                S = T[8*rr:8*rr+8, 0:128]
                h = lax.rsqrt(S)
                e = h*h*h
                acc = [acc[c]+e*T[8*rr:8*rr+8, 128*(c+1):128*(c+2)] for c in range(3)]
            prep_leaf(src(k), k, ns, *cs)
        for c in range(3):
            total = jnp.sum(acc[c], axis=0, keepdims=True)*WSC
            if near:
                out_ref[c:c+1, lanes(t)] = total
            else:
                out_ref[c:c+1, lanes(t)] += jnp.where(i < count, total, 0.0)

    prep_all(0, 0)

    def steps(many, start, stop):
        def body(i, _):
            for j in range(many):
                step(start + many*i + j, j % 2)
            return 0
        lax.fori_loop(0, lax.div(stop - start + many - 1, many), body, 0)
    if near:
        steps(4, 0, count)
    else:
        most = count & ~7
        steps(8, 0, most)
        steps(2, most, count)


VM = pl.BlockSpec(memory_space=pltpu.VMEM)
SM = pl.BlockSpec(memory_space=pltpu.SMEM)


def pairs(mode, n_src, scalars, arrays):
    n = arrays[0].shape[1] // 128
    return pl.pallas_call(
        functools.partial(pair_kernel, mode, n_src),
        out_shape=jax.ShapeDtypeStruct((3, n*128), f32),
        in_specs=[SM]*len(scalars)+[VM]*len(arrays), out_specs=VM,
        scratch_shapes=[
            pltpu.VMEM((2, 128, 512), bf16), pltpu.VMEM((n, 8, 128), f32),
            pltpu.VMEM((n if mode == "near" else n_src, 48, 128), f32), pltpu.VMEM((24, 8, 128), f32),
            pltpu.VMEM((2, n_src*128, 128), bf16)],
        name=mode, cost_estimate=pl.CostEstimate(flops=COST[mode], bytes_accessed=1000000, transcendentals=0),
        compiler_params=pltpu.CompilerParams(vmem_limit_bytes=40 << 20),
    )(*scalars, *arrays)


COST = {"near": 20000000000, "first": 16000000000, "rest": 6000000000}


def request_kernel(owner_ref, slot_ref, y_ref, f_ref, want_ref, plan_ref, own_ref):
    pack(y_ref, f_ref, own_ref)
    far, rows = owner_ref.shape
    groups = want_ref.shape[0]
    my_y, my_core = lax.axis_index("y"), lax.axis_index("core")
    group = lax.broadcasted_iota(jnp.int32, (groups, rows), 0)
    hits = [jnp.where(lax.shift_right_logical(owner_ref[k:k+1, :], 3) == group, 1.0, 0.0) for k in range(far)]
    named = hits[0]
    for k in range(1, far):
        named = named + hits[k]
    before = lax.broadcasted_iota(jnp.int32, (rows, rows), 0) < lax.broadcasted_iota(jnp.int32, (rows, rows), 1)
    rank = jnp.dot(named.astype(bf16), before.astype(f32).astype(bf16), preferred_element_type=f32)
    place = lax.broadcasted_iota(jnp.int32, (128, rows), 0)
    want = jnp.zeros((groups, 128), f32)
    mine = []
    for k in range(far):
        own = jnp.sum(hits[k]*rank, axis=0, keepdims=True).astype(jnp.int32)
        rank = rank + hits[k]
        mine.append(own)
        o = owner_ref[k:k+1, :]
        dy = (lax.shift_right_logical(o, 1) - my_y) & 3
        dc = (o - my_core) & 1
        value = (dy*64 + dc*32 + slot_ref[k:k+1, :]).astype(f32)
        at = jnp.where(place == own, value, 0.0)
        want = want + lax.dot_general(hits[k].astype(bf16), at.astype(bf16), (((1,), (1,)), ((), ())),
                                      preferred_element_type=f32)
    want_ref[...] = want.astype(jnp.int32)
    base = []
    for k in range(far):
        asked = lax.shift_right_logical(owner_ref[k:k+1, :], 3)
        late = groups*PER_A + asked*PER_B + (mine[k]-FIRST)*6
        base.append(jnp.where(mine[k] >= FIRST, late, asked*PER_A + mine[k]*6))
    order = []
    for k in range(far):
        p = jnp.zeros((1, rows), jnp.int32)
        for j in range(far):
            if j != k:
                p = p + jnp.where((mine[j] < mine[k]) if j > k else (mine[j] <= mine[k]), 1, 0)
        order.append(p)
    plan_ref[...] = jnp.zeros(plan_ref.shape, jnp.int32)
    tops = []
    for p in range(far):
        b = jnp.zeros((1, rows), jnp.int32)
        m = jnp.zeros((1, rows), jnp.int32)
        for k in range(far):
            b = b + jnp.where(order[k] == p, base[k], 0)
            if p % UNIT == UNIT-1:
                m = m + jnp.where(order[k] == p, mine[k], 0)
        plan_ref[p:p+1, 0:rows] = b
        if p % UNIT == UNIT-1:
            tops.append(m)
    top = jnp.concatenate(tops + [jnp.full((1, 128 - 2*rows), CAP, jnp.int32)], 1)
    unit = lax.broadcasted_iota(jnp.int32, (1, 128), 1)
    ready = jnp.where((top < FIRST) & (unit < 2*rows), 1.0, 0.0)
    lower = lax.broadcasted_iota(jnp.int32, (128, 128), 0) < lax.broadcasted_iota(jnp.int32, (128, 128), 1)
    ahead = jnp.dot(jnp.broadcast_to(ready, (8, 128)).astype(bf16), lower.astype(f32).astype(bf16),
                    preferred_element_type=f32)[0:1]
    count = jnp.sum(ready, axis=1, keepdims=True)
    spot = jnp.where(ready > 0.0, ahead, count + unit.astype(f32) - ahead)
    spot = jnp.transpose(jnp.broadcast_to(spot, (128, 128)))
    row = lax.broadcasted_iota(jnp.int32, (128, 128), 0)
    lane = lax.broadcasted_iota(jnp.int32, (128, 128), 1).astype(f32)
    listed = jnp.sum(jnp.where((spot == lane) & (row < 2*rows), row.astype(f32), 0.0), axis=0, keepdims=True)
    plan_ref[far:far+1, :] = listed.astype(jnp.int32)
    plan_ref[far+1:far+2, :] = jnp.broadcast_to(count, (1, 128)).astype(jnp.int32)


def pack(y_ref, f_ref, out_ref):
    for t in range(y_ref.shape[1] // 128):
        out_ref[8*t:8*t+3, :] = y_ref[:, 128*t:128*t+128]
        out_ref[8*t+3:8*t+6, :] = f_ref[:, 128*t:128*t+128]
        out_ref[8*t+6:8*t+8, :] = jnp.zeros((2, 128), f32)


def reply_kernel(ranks, *refs):
    ask_ref, *tables = refs[:5]
    out_ref, table_ref = refs[-2:]
    rows = tables[0].shape[0]
    for i, ref in enumerate(tables):
        table_ref[rows*i:rows*i+rows, :] = ref[...]

    def one(p, _):
        for q, r in enumerate(ranks):
            tile = table_ref[pl.ds(pl.multiple_of(ask_ref[p, r] * 8, 8), 8), :]
            out_ref[p, 6*q:6*q+6, :] = tile[0:6]
        return 0
    lax.fori_loop(0, out_ref.shape[0], one, 0)


def per_device(points, forces, near_leaf, far_owner, far_slot):
    n, near_count = near_leaf.shape
    far_count = far_owner.shape[1]
    groups = lax.axis_size("seg")
    i32 = jnp.int32
    want, plan, own = pl.pallas_call(
        request_kernel,
        out_shape=(jax.ShapeDtypeStruct((groups, 128), i32), jax.ShapeDtypeStruct((far_count + 2, 128), i32),
                   jax.ShapeDtypeStruct((8*n, 128), f32)),
        in_specs=[VM]*4, out_specs=(VM, VM, VM), name="requests",
    )(far_owner.T, far_slot.T, points, forces)

    def send(values):
        return lax.all_to_all(values, "seg", split_axis=0, concat_axis=0, tiled=True)
    asked = send(want.reshape(groups, 1, 128)).reshape(groups, 128)

    chip = jnp.concatenate([own, lax.ppermute(own, "core", [(0, 1), (1, 0)])], 0)
    tables = [chip] + [lax.ppermute(chip, "y", [(i, (i - d) % 4) for i in range(4)]) for d in (1, 2, 3)]

    def answer(ranks, *after):
        reply = pl.pallas_call(
            functools.partial(reply_kernel, ranks),
            out_shape=jax.ShapeDtypeStruct((groups, 6*len(ranks), 128), f32),
            in_specs=[SM] + [VM]*(4 + len(after)), out_specs=VM,
            scratch_shapes=[pltpu.VMEM((64*n, 128), f32)], name="replies",
            compiler_params=pltpu.CompilerParams(vmem_limit_bytes=32 << 20),
        )(asked, *tables, *after)
        return reply, send(reply).reshape(-1, 128)
    reply_a, answers_a = answer(range(0, FIRST))
    near = pairs("near", near_count, (near_leaf.T, asked), (points, forces))
    reply_b, answers_b = answer(range(FIRST, CAP), near)
    first = pairs("first", UNIT, (plan,), (points, near, answers_a))
    return pairs("rest", UNIT, (plan,), (points, first, answers_a, answers_b))


def solution(mesh):
    grid = jax.sharding.Mesh(mesh.devices.reshape(mesh.devices.shape[0], -1, 2), ("seg", "y", "core"))
    every = ("seg", "y", "core")
    split = P(None, every)
    rows = P(every, None)
    return jax.shard_map(
        per_device, mesh=grid, in_specs=(split, split, rows, rows, rows), out_specs=split, check_vma=False
    )
```

```python
import functools
import math

import jax
import jax.numpy as jnp
from jax import lax
from jax.experimental import pallas as pl
from jax.experimental.pallas import tpu as pltpu
from jax.sharding import PartitionSpec as P

A = 1.0 / (4.0 * math.pi)
B = A / (4.0 * (1.0 - 0.3))
E = 0.05
C1 = A - B
C2 = A * E * E / 2
K2 = C1 / C2
WSC = C1 * math.sqrt(K2)
QK = B / C1 * K2
KE = K2 * E * E
CAP = 56
FIRST = 30
PER_A = 184
PER_B = 160
UNIT = 7
f32 = jnp.float32
bf16 = jnp.bfloat16
PA=['y0','y1','y2','f0','f1','f2','y0','y0','y0','y1','y1','y1','y2','y2','y2',None]
PB=[None]*6+['f0','f1','f2','f0','f1','f2','f0','f1','f2',None]
PC=[None,'f0','f1','f2']*2
PD=[None,'y0','y1','y2']*2
ROWS=PA+PB+PC+PD
NEED={n:[i for i,r in enumerate(ROWS) if r==n] for n in ('y0','y1','y2','f0','f1','f2')}
NAMES=('y0','y1','y2','f0','f1','f2')

def split3(v):
    a=v.astype(bf16); r=v-a.astype(f32)
    b=r.astype(bf16); r=r-b.astype(f32)
    return a,b,r.astype(bf16)

def lin_coef(table,row):
    co=[0.0]*3
    if table==0:
        if row<3: co[row]=-2.0*K2
        return co
    i=table-1
    if 6<=row<15:
        a,b=divmod(row-6,3)
        if i==b: co[a]-=2.0*K2
        if i==a: co[b]-=QK
        if a==b: co[i]-=QK
    return co

def const_rows(vals):
    r=lax.broadcasted_iota(jnp.int32,(8,128),0)
    v=jnp.full((8,128),vals[0],f32)
    for k in range(1,8): v=jnp.where(r==k,vals[k],v)
    return v

def pair_kernel(mode, n_src, *refs):
    near = mode == "near"
    w_ref, cen_ref, st_ref, co_ref, lhs_ref = refs[-5:]
    out_ref = refs[-6]
    if near:
        idx_ref, _, y_ref, f_ref = refs[:4]
    elif mode == "first":
        idx_ref, y_ref, part_ref, a_ref = refs[:4]
    else:
        idx_ref, y_ref, part_ref, a_ref, b_ref = refs[:5]
    n = y_ref.shape[1] // 128

    def lanes(s):
        return pl.ds(pl.multiple_of(s * 128, 128), 128)

    def fetch(s):
        if near:
            return [y_ref[c:c+1, lanes(s)] for c in range(3)] + [f_ref[c:c+1, lanes(s)] for c in range(3)]
        last = a_ref.shape[0] - 6
        if mode == "first":
            s = jnp.minimum(s, last)
            return [a_ref[pl.ds(s + c, 1), :] for c in range(6)]
        late = s > last
        sa = jnp.where(late, 0, s)
        sb = jnp.where(late, s - a_ref.shape[0], 0)
        return [jnp.where(late, b_ref[pl.ds(sb + c, 1), :], a_ref[pl.ds(sa + c, 1), :]) for c in range(6)]

    for t in range(n):
        v = y_ref[:, 128*t:128*t+128]
        cen_ref[t, 0:3, :] = jnp.broadcast_to(jnp.mean(v, axis=1, keepdims=True), (3, 128))
    for T in range(4):
        for H in range(2):
            for a in range(3):
                co_ref[(T*2+H)*3+a] = const_rows([lin_coef(T, 8*H+r)[a] for r in range(8)])

    def fill(l, rows):
        for c, nm in enumerate(NAMES):
            for i in NEED[nm]:
                st_ref[l, i:i+1, :] = rows[c]

    def init(l, _):
        st_ref[l] = jnp.ones((48, 128), f32)
        if near:
            fill(l, fetch(l))
        return 0
    lax.fori_loop(0, st_ref.shape[0], init, 0)

    sub = lax.broadcasted_iota(jnp.int32, (8, 128), 0)
    r16 = lax.broadcasted_iota(jnp.int32, (16, 512), 0)
    l16 = lax.broadcasted_iota(jnp.int32, (16, 512), 1) // 128
    wone = jnp.where((r16 < 12) & (r16 % 4 == l16), 1.0, 0.0).astype(bf16)
    for sl in range(2):
        w_ref[sl, 96:112, :] = wone
        w_ref[sl, 112:128, :] = jnp.zeros((16, 512), bf16)

    if near:
        count = n
    else:
        out_ref[...] = part_ref[...]

        units = 2*UNIT
        ready = idx_ref[units + 1, 0]
        first_unit = 0 if mode == "first" else ready
        count = ready if mode == "first" else 2*n - ready

    def place(i):
        if near:
            t = jnp.minimum(i, n - 1)
            return t, lambda k: idx_ref[k, t]
        u = idx_ref[units, first_unit + jnp.maximum(jnp.minimum(i, count - 1), 0)]
        t = u & 31
        half = lax.shift_right_logical(u, 5) * UNIT
        return t, lambda k: idx_ref[half + k, t]

    def prep_w(t, slot):
        x = [jnp.broadcast_to(y_ref[c:c+1, lanes(t)] - cen_ref[t, c:c+1, :], (8, 128)) for c in range(3)]
        xx = K2*(x[0]*x[0]+x[1]*x[1]+x[2]*x[2])
        xj = QK*jnp.where(sub == 3, x[0], jnp.where(sub == 4, x[1], jnp.where(sub == 5, x[2], 0.0)))
        for T in range(4):
            hs = []
            for H in range(2):
                v = None
                for a in range(3):
                    if any(lin_coef(T, 8*H+r)[a] != 0 for r in range(8)):
                        w = co_ref[(T*2+H)*3+a]*x[a]
                        v = w if v is None else v+w
                if v is None:
                    v = jnp.zeros((8, 128), f32)
                if T == 0 and H == 1:
                    v = jnp.where(sub == 7, xx, v)
                if T > 0 and H == 0:
                    v = v+x[T-1]*xj+jnp.where(sub == 2+T, xx, 0.0)
                hs.append(v)
            b1, b2, b3 = split3(jnp.concatenate(hs, 0))
            ls = slice(128*T, 128*T+128)
            for blk, b in enumerate((b1, b2, b3, b1, b2, b1)):
                w_ref[slot, 16*blk:16*blk+16, ls] = b

    def prep_leaf(s, k, slot, cenA, cenD, cen):
        rows = fetch(s)
        if near:
            l = s
        else:
            l = k
            fill(l, rows)
        y = [jnp.broadcast_to(rows[c], (8, 128))-cen[c] for c in range(3)]
        f = [jnp.broadcast_to(rows[3+c], (8, 128)) for c in range(3)]
        Y = K2*(y[0]*y[0]+y[1]*y[1]+y[2]*y[2])+jnp.where(sub % 4 == 0, KE, KE+1.0)
        yf = QK*(y[0]*f[0]+y[1]*f[1]+y[2]*f[2])
        t48 = st_ref[l]
        V = (t48[0:16]-cenA)*t48[16:32]
        C = t48[32:40]*Y+yf*(t48[40:48]-cenD)
        C = jnp.where(sub % 4 == 0, Y, C)
        a, b, c = split3(V)
        p = C.astype(bf16).astype(f32)
        r = C-p
        o = r.astype(bf16).astype(f32)
        r = r-o
        cc = jnp.concatenate([jnp.where(sub < 4, p, o), jnp.where(sub < 4, r, 0.0)], 0).astype(bf16)
        at = jnp.concatenate([a, a, a, b, b, c, cc, cc], 0)
        lhs_ref[slot, 128*k:128*k+128, :] = jnp.transpose(at)

    def cens(t):
        cen = [jnp.broadcast_to(cen_ref[t, c:c+1, :], (8, 128)) for c in range(3)]

        def pat(rows):
            v = jnp.zeros((8, 128), f32)
            for c in range(3):
                for k, nm in enumerate(rows):
                    if nm == "y%d" % c:
                        v = jnp.where(sub == k, cen[c], v)
            return v
        return jnp.concatenate([pat(PA[:8]), pat(PA[8:])], 0), pat(PD), cen

    def prep_all(i, slot):
        t, src = place(i)
        prep_w(t, slot)
        cs = cens(t)
        for k in range(n_src):
            prep_leaf(src(k), k, slot, *cs)

    def step(i, slot):
        t, _ = place(i)
        tn, src = place(i + 1)
        ns = 1-slot
        T = lax.dot_general(lhs_ref[slot], w_ref[slot], (((1,), (0,)), ((), ())), preferred_element_type=f32)
        cs = cens(tn)
        acc = [jnp.zeros((8, 128), f32) for _ in range(3)]
        prep_w(tn, ns)
        for k in range(n_src):
            for rr in range(16*k, 16*k+16):
                S = T[8*rr:8*rr+8, 0:128]
                h = lax.rsqrt(S)
                e = h*h*h
                acc = [acc[c]+e*T[8*rr:8*rr+8, 128*(c+1):128*(c+2)] for c in range(3)]
            prep_leaf(src(k), k, ns, *cs)
        for c in range(3):
            total = jnp.sum(acc[c], axis=0, keepdims=True)*WSC
            if near:
                out_ref[c:c+1, lanes(t)] = total
            else:
                out_ref[c:c+1, lanes(t)] += jnp.where(i < count, total, 0.0)

    prep_all(0, 0)

    def steps(many, start, stop):
        def body(i, _):
            for j in range(many):
                step(start + many*i + j, j % 2)
            return 0
        lax.fori_loop(0, lax.div(stop - start + many - 1, many), body, 0)
    if near:
        steps(8, 0, count)
    else:
        most = count & ~7
        steps(8, 0, most)
        steps(2, most, count)


VM = pl.BlockSpec(memory_space=pltpu.VMEM)
SM = pl.BlockSpec(memory_space=pltpu.SMEM)


def pairs(mode, n_src, scalars, arrays):
    n = arrays[0].shape[1] // 128
    return pl.pallas_call(
        functools.partial(pair_kernel, mode, n_src),
        out_shape=jax.ShapeDtypeStruct((3, n*128), f32),
        in_specs=[SM]*len(scalars)+[VM]*len(arrays), out_specs=VM,
        scratch_shapes=[
            pltpu.VMEM((2, 128, 512), bf16), pltpu.VMEM((n, 8, 128), f32),
            pltpu.VMEM((n if mode == "near" else n_src, 48, 128), f32), pltpu.VMEM((24, 8, 128), f32),
            pltpu.VMEM((2, n_src*128, 128), bf16)],
        name=mode, cost_estimate=pl.CostEstimate(flops=COST[mode], bytes_accessed=1000000, transcendentals=0),
        compiler_params=pltpu.CompilerParams(vmem_limit_bytes=40 << 20),
    )(*scalars, *arrays)


COST = {"near": 20000000000, "first": 16000000000, "rest": 6000000000}


def request_kernel(owner_ref, slot_ref, y_ref, f_ref, want_ref, plan_ref, own_ref):
    pack(y_ref, f_ref, own_ref)
    far, rows = owner_ref.shape
    groups = want_ref.shape[0]
    my_y, my_core = lax.axis_index("y"), lax.axis_index("core")
    group = lax.broadcasted_iota(jnp.int32, (groups, rows), 0)
    hits = [jnp.where(lax.shift_right_logical(owner_ref[k:k+1, :], 3) == group, 1.0, 0.0) for k in range(far)]
    named = hits[0]
    for k in range(1, far):
        named = named + hits[k]
    before = lax.broadcasted_iota(jnp.int32, (rows, rows), 0) < lax.broadcasted_iota(jnp.int32, (rows, rows), 1)
    rank = jnp.dot(named.astype(bf16), before.astype(f32).astype(bf16), preferred_element_type=f32)
    place = lax.broadcasted_iota(jnp.int32, (128, rows), 0)
    want = jnp.zeros((groups, 128), f32)
    mine = []
    for k in range(far):
        own = jnp.sum(hits[k]*rank, axis=0, keepdims=True).astype(jnp.int32)
        rank = rank + hits[k]
        mine.append(own)
        o = owner_ref[k:k+1, :]
        dy = (lax.shift_right_logical(o, 1) - my_y) & 3
        dc = (o - my_core) & 1
        value = (dy*64 + dc*32 + slot_ref[k:k+1, :]).astype(f32)
        at = jnp.where(place == own, value, 0.0)
        want = want + lax.dot_general(hits[k].astype(bf16), at.astype(bf16), (((1,), (1,)), ((), ())),
                                      preferred_element_type=f32)
    want_ref[...] = want.astype(jnp.int32)
    base = []
    for k in range(far):
        asked = lax.shift_right_logical(owner_ref[k:k+1, :], 3)
        late = groups*PER_A + asked*PER_B + (mine[k]-FIRST)*6
        base.append(jnp.where(mine[k] >= FIRST, late, asked*PER_A + mine[k]*6))
    order = []
    for k in range(far):
        p = jnp.zeros((1, rows), jnp.int32)
        for j in range(far):
            if j != k:
                p = p + jnp.where((mine[j] < mine[k]) if j > k else (mine[j] <= mine[k]), 1, 0)
        order.append(p)
    plan_ref[...] = jnp.zeros(plan_ref.shape, jnp.int32)
    tops = []
    for p in range(far):
        b = jnp.zeros((1, rows), jnp.int32)
        m = jnp.zeros((1, rows), jnp.int32)
        for k in range(far):
            b = b + jnp.where(order[k] == p, base[k], 0)
            if p % UNIT == UNIT-1:
                m = m + jnp.where(order[k] == p, mine[k], 0)
        plan_ref[p:p+1, 0:rows] = b
        if p % UNIT == UNIT-1:
            tops.append(m)
    top = jnp.concatenate(tops + [jnp.full((1, 128 - 2*rows), CAP, jnp.int32)], 1)
    unit = lax.broadcasted_iota(jnp.int32, (1, 128), 1)
    ready = jnp.where((top < FIRST) & (unit < 2*rows), 1.0, 0.0)
    lower = lax.broadcasted_iota(jnp.int32, (128, 128), 0) < lax.broadcasted_iota(jnp.int32, (128, 128), 1)
    ahead = jnp.dot(jnp.broadcast_to(ready, (8, 128)).astype(bf16), lower.astype(f32).astype(bf16),
                    preferred_element_type=f32)[0:1]
    count = jnp.sum(ready, axis=1, keepdims=True)
    spot = jnp.where(ready > 0.0, ahead, count + unit.astype(f32) - ahead)
    spot = jnp.transpose(jnp.broadcast_to(spot, (128, 128)))
    row = lax.broadcasted_iota(jnp.int32, (128, 128), 0)
    lane = lax.broadcasted_iota(jnp.int32, (128, 128), 1).astype(f32)
    listed = jnp.sum(jnp.where((spot == lane) & (row < 2*rows), row.astype(f32), 0.0), axis=0, keepdims=True)
    plan_ref[far:far+1, :] = listed.astype(jnp.int32)
    plan_ref[far+1:far+2, :] = jnp.broadcast_to(count, (1, 128)).astype(jnp.int32)


def pack(y_ref, f_ref, out_ref):
    for t in range(y_ref.shape[1] // 128):
        out_ref[6*t:6*t+3, :] = y_ref[:, 128*t:128*t+128]
        out_ref[6*t+3:6*t+6, :] = f_ref[:, 128*t:128*t+128]


def reply_kernel(ranks, *refs):
    ask_ref, *tables = refs[:5]
    out_ref, table_ref = refs[-2:]
    leaves = tables[0].shape[0] // 6
    for i, ref in enumerate(tables):
        for k in range(leaves):
            to = 8*(leaves*i + k)
            table_ref[to:to+6, :] = ref[6*k:6*k+6, :]

    def one(p, _):
        for q, r in enumerate(ranks):
            tile = table_ref[pl.ds(pl.multiple_of(ask_ref[p, r] * 8, 8), 8), :]
            out_ref[p, 6*q:6*q+6, :] = tile[0:6]
        return 0
    lax.fori_loop(0, out_ref.shape[0], one, 0)


def per_device(points, forces, near_leaf, far_owner, far_slot):
    n, near_count = near_leaf.shape
    far_count = far_owner.shape[1]
    groups = lax.axis_size("seg")
    i32 = jnp.int32
    want, plan, own = pl.pallas_call(
        request_kernel,
        out_shape=(jax.ShapeDtypeStruct((groups, 128), i32), jax.ShapeDtypeStruct((far_count + 2, 128), i32),
                   jax.ShapeDtypeStruct((6*n, 128), f32)),
        in_specs=[VM]*4, out_specs=(VM, VM, VM), name="requests",
    )(far_owner.T, far_slot.T, points, forces)

    def send(values):
        return lax.all_to_all(values, "seg", split_axis=0, concat_axis=0, tiled=True)
    asked = send(want.reshape(groups, 1, 128)).reshape(groups, 128)

    chip = jnp.concatenate([own, lax.ppermute(own, "core", [(0, 1), (1, 0)])], 0)
    tables = [chip] + [lax.ppermute(chip, "y", [(i, (i - d) % 4) for i in range(4)]) for d in (1, 2, 3)]

    def answer(per, ranks, *after):
        reply = pl.pallas_call(
            functools.partial(reply_kernel, ranks),
            out_shape=jax.ShapeDtypeStruct((groups, per, 128), f32),
            in_specs=[SM] + [VM]*(4 + len(after)), out_specs=VM,
            scratch_shapes=[pltpu.VMEM((64*n, 128), f32)], name="replies",
            compiler_params=pltpu.CompilerParams(vmem_limit_bytes=32 << 20),
        )(asked, *tables, *after)
        return reply, send(reply).reshape(-1, 128)
    reply_a, answers_a = answer(PER_A, range(0, FIRST))
    near = pairs("near", near_count, (near_leaf.T, asked), (points, forces))
    reply_b, answers_b = answer(PER_B, range(FIRST, CAP), near)
    first = pairs("first", UNIT, (plan,), (points, near, answers_a))
    return pairs("rest", UNIT, (plan,), (points, first, answers_a, answers_b))


def solution(mesh):
    grid = jax.sharding.Mesh(mesh.devices.reshape(mesh.devices.shape[0], -1, 2), ("seg", "y", "core"))
    every = ("seg", "y", "core")
    split = P(None, every)
    rows = P(every, None)
    return jax.shard_map(
        per_device, mesh=grid, in_specs=(split, split, rows, rows, rows), out_specs=split, check_vma=False
    )
```

```python
import functools
import math

import jax
import jax.numpy as jnp
from jax import lax
from jax.experimental import pallas as pl
from jax.experimental.pallas import tpu as pltpu
from jax.sharding import PartitionSpec as P

A = 1.0 / (4.0 * math.pi)
B = A / (4.0 * (1.0 - 0.3))
E = 0.05
C1 = A - B
C2 = A * E * E / 2
K2 = C1 / C2
WSC = C1 * math.sqrt(K2)
QK = B / C1 * K2
KE = K2 * E * E
CAP = 56
FIRST = 32
PER_A = 192
PER_B = 144
UNIT = 7
f32 = jnp.float32
bf16 = jnp.bfloat16
PA=['y0','y1','y2','f0','f1','f2','y0','y0','y0','y1','y1','y1','y2','y2','y2',None]
PB=[None]*6+['f0','f1','f2','f0','f1','f2','f0','f1','f2',None]
PC=[None,'f0','f1','f2']*2
PD=[None,'y0','y1','y2']*2
ROWS=PA+PB+PC+PD
NEED={n:[i for i,r in enumerate(ROWS) if r==n] for n in ('y0','y1','y2','f0','f1','f2')}
NAMES=('y0','y1','y2','f0','f1','f2')

def split3(v):
    a=v.astype(bf16); r=v-a.astype(f32)
    b=r.astype(bf16); r=r-b.astype(f32)
    return a,b,r.astype(bf16)

def lin_coef(table,row):
    co=[0.0]*3
    if table==0:
        if row<3: co[row]=-2.0*K2
        return co
    i=table-1
    if 6<=row<15:
        a,b=divmod(row-6,3)
        if i==b: co[a]-=2.0*K2
        if i==a: co[b]-=QK
        if a==b: co[i]-=QK
    return co

def const_rows(vals):
    r=lax.broadcasted_iota(jnp.int32,(8,128),0)
    v=jnp.full((8,128),vals[0],f32)
    for k in range(1,8): v=jnp.where(r==k,vals[k],v)
    return v

def pair_kernel(mode, n_src, *refs):
    near = mode == "near"
    w_ref, cen_ref, st_ref, co_ref, lhs_ref = refs[-5:]
    out_ref = refs[-6]
    if near:
        idx_ref, _, y_ref, f_ref = refs[:4]
    elif mode == "first":
        idx_ref, y_ref, part_ref, a_ref = refs[:4]
    else:
        idx_ref, y_ref, part_ref, a_ref, b_ref = refs[:5]
    n = y_ref.shape[1] // 128

    def lanes(s):
        return pl.ds(pl.multiple_of(s * 128, 128), 128)

    def fetch(s):
        if near:
            return [y_ref[c:c+1, lanes(s)] for c in range(3)] + [f_ref[c:c+1, lanes(s)] for c in range(3)]
        last = a_ref.shape[0] - 6
        if mode == "first":
            s = jnp.minimum(s, last)
            return [a_ref[pl.ds(s + c, 1), :] for c in range(6)]
        late = s > last
        sa = jnp.where(late, 0, s)
        sb = jnp.where(late, s - a_ref.shape[0], 0)
        return [jnp.where(late, b_ref[pl.ds(sb + c, 1), :], a_ref[pl.ds(sa + c, 1), :]) for c in range(6)]

    for t in range(n):
        v = y_ref[:, 128*t:128*t+128]
        cen_ref[t, 0:3, :] = jnp.broadcast_to(jnp.mean(v, axis=1, keepdims=True), (3, 128))
    for T in range(4):
        for H in range(2):
            for a in range(3):
                co_ref[(T*2+H)*3+a] = const_rows([lin_coef(T, 8*H+r)[a] for r in range(8)])

    def fill(l, rows):
        for c, nm in enumerate(NAMES):
            for i in NEED[nm]:
                st_ref[l, i:i+1, :] = rows[c]

    def init(l, _):
        st_ref[l] = jnp.ones((48, 128), f32)
        if near:
            fill(l, fetch(l))
        return 0
    lax.fori_loop(0, st_ref.shape[0], init, 0)

    sub = lax.broadcasted_iota(jnp.int32, (8, 128), 0)
    r16 = lax.broadcasted_iota(jnp.int32, (16, 512), 0)
    l16 = lax.broadcasted_iota(jnp.int32, (16, 512), 1) // 128
    wone = jnp.where((r16 < 12) & (r16 % 4 == l16), 1.0, 0.0).astype(bf16)
    for sl in range(2):
        w_ref[sl, 96:112, :] = wone
        w_ref[sl, 112:128, :] = jnp.zeros((16, 512), bf16)

    if near:
        count = n
    else:
        out_ref[...] = part_ref[...]

        units = 2*UNIT
        ready = idx_ref[units + 1, 0]
        first_unit = 0 if mode == "first" else ready
        count = ready if mode == "first" else 2*n - ready

    def place(i):
        if near:
            t = jnp.minimum(i, n - 1)
            return t, lambda k: idx_ref[k, t]
        u = idx_ref[units, first_unit + jnp.maximum(jnp.minimum(i, count - 1), 0)]
        t = u & 31
        half = lax.shift_right_logical(u, 5) * UNIT
        return t, lambda k: idx_ref[half + k, t]

    def prep_w(t, slot):
        x = [jnp.broadcast_to(y_ref[c:c+1, lanes(t)] - cen_ref[t, c:c+1, :], (8, 128)) for c in range(3)]
        xx = K2*(x[0]*x[0]+x[1]*x[1]+x[2]*x[2])
        xj = QK*jnp.where(sub == 3, x[0], jnp.where(sub == 4, x[1], jnp.where(sub == 5, x[2], 0.0)))
        for T in range(4):
            hs = []
            for H in range(2):
                v = None
                for a in range(3):
                    if any(lin_coef(T, 8*H+r)[a] != 0 for r in range(8)):
                        w = co_ref[(T*2+H)*3+a]*x[a]
                        v = w if v is None else v+w
                if v is None:
                    v = jnp.zeros((8, 128), f32)
                if T == 0 and H == 1:
                    v = jnp.where(sub == 7, xx, v)
                if T > 0 and H == 0:
                    v = v+x[T-1]*xj+jnp.where(sub == 2+T, xx, 0.0)
                hs.append(v)
            b1, b2, b3 = split3(jnp.concatenate(hs, 0))
            ls = slice(128*T, 128*T+128)
            for blk, b in enumerate((b1, b2, b3, b1, b2, b1)):
                w_ref[slot, 16*blk:16*blk+16, ls] = b

    def prep_leaf(s, k, slot, cenA, cenD, cen):
        rows = fetch(s)
        if near:
            l = s
        else:
            l = k
            fill(l, rows)
        y = [jnp.broadcast_to(rows[c], (8, 128))-cen[c] for c in range(3)]
        f = [jnp.broadcast_to(rows[3+c], (8, 128)) for c in range(3)]
        Y = K2*(y[0]*y[0]+y[1]*y[1]+y[2]*y[2])+jnp.where(sub % 4 == 0, KE, KE+1.0)
        yf = QK*(y[0]*f[0]+y[1]*f[1]+y[2]*f[2])
        t48 = st_ref[l]
        V = (t48[0:16]-cenA)*t48[16:32]
        C = t48[32:40]*Y+yf*(t48[40:48]-cenD)
        C = jnp.where(sub % 4 == 0, Y, C)
        a, b, c = split3(V)
        p = C.astype(bf16).astype(f32)
        r = C-p
        o = r.astype(bf16).astype(f32)
        r = r-o
        cc = jnp.concatenate([jnp.where(sub < 4, p, o), jnp.where(sub < 4, r, 0.0)], 0).astype(bf16)
        at = jnp.concatenate([a, a, a, b, b, c, cc, cc], 0)
        lhs_ref[slot, 128*k:128*k+128, :] = jnp.transpose(at)

    def cens(t):
        cen = [jnp.broadcast_to(cen_ref[t, c:c+1, :], (8, 128)) for c in range(3)]

        def pat(rows):
            v = jnp.zeros((8, 128), f32)
            for c in range(3):
                for k, nm in enumerate(rows):
                    if nm == "y%d" % c:
                        v = jnp.where(sub == k, cen[c], v)
            return v
        return jnp.concatenate([pat(PA[:8]), pat(PA[8:])], 0), pat(PD), cen

    def prep_all(i, slot):
        t, src = place(i)
        prep_w(t, slot)
        cs = cens(t)
        for k in range(n_src):
            prep_leaf(src(k), k, slot, *cs)

    def step(i, slot):
        t, _ = place(i)
        tn, src = place(i + 1)
        ns = 1-slot
        T = lax.dot_general(lhs_ref[slot], w_ref[slot], (((1,), (0,)), ((), ())), preferred_element_type=f32)
        cs = cens(tn)
        acc = [jnp.zeros((8, 128), f32) for _ in range(3)]
        prep_w(tn, ns)
        for k in range(n_src):
            for rr in range(16*k, 16*k+16):
                S = T[8*rr:8*rr+8, 0:128]
                h = lax.rsqrt(S)
                e = h*h*h
                acc = [acc[c]+e*T[8*rr:8*rr+8, 128*(c+1):128*(c+2)] for c in range(3)]
            prep_leaf(src(k), k, ns, *cs)
        for c in range(3):
            total = jnp.sum(acc[c], axis=0, keepdims=True)*WSC
            if near:
                out_ref[c:c+1, lanes(t)] = total
            else:
                out_ref[c:c+1, lanes(t)] += jnp.where(i < count, total, 0.0)

    prep_all(0, 0)

    def steps(many, start, stop):
        def body(i, _):
            for j in range(many):
                step(start + many*i + j, j % 2)
            return 0
        lax.fori_loop(0, lax.div(stop - start + many - 1, many), body, 0)
    if near:
        steps(8, 0, count)
    else:
        most = count & ~7
        steps(8, 0, most)
        steps(2, most, count)


VM = pl.BlockSpec(memory_space=pltpu.VMEM)
SM = pl.BlockSpec(memory_space=pltpu.SMEM)


def pairs(mode, n_src, scalars, arrays):
    n = arrays[0].shape[1] // 128
    return pl.pallas_call(
        functools.partial(pair_kernel, mode, n_src),
        out_shape=jax.ShapeDtypeStruct((3, n*128), f32),
        in_specs=[SM]*len(scalars)+[VM]*len(arrays), out_specs=VM,
        scratch_shapes=[
            pltpu.VMEM((2, 128, 512), bf16), pltpu.VMEM((n, 8, 128), f32),
            pltpu.VMEM((n if mode == "near" else n_src, 48, 128), f32), pltpu.VMEM((24, 8, 128), f32),
            pltpu.VMEM((2, n_src*128, 128), bf16)],
        name=mode, cost_estimate=pl.CostEstimate(flops=COST[mode], bytes_accessed=1000000, transcendentals=0),
        compiler_params=pltpu.CompilerParams(vmem_limit_bytes=40 << 20),
    )(*scalars, *arrays)


COST = {"near": 20000000000, "first": 16000000000, "rest": 6000000000}


def request_kernel(owner_ref, slot_ref, y_ref, f_ref, want_ref, plan_ref, own_ref):
    pack(y_ref, f_ref, own_ref)
    far, rows = owner_ref.shape
    groups = want_ref.shape[0]
    my_y, my_core = lax.axis_index("y"), lax.axis_index("core")
    group = lax.broadcasted_iota(jnp.int32, (groups, rows), 0)
    hits = [jnp.where(lax.shift_right_logical(owner_ref[k:k+1, :], 3) == group, 1.0, 0.0) for k in range(far)]
    named = hits[0]
    for k in range(1, far):
        named = named + hits[k]
    before = lax.broadcasted_iota(jnp.int32, (rows, rows), 0) < lax.broadcasted_iota(jnp.int32, (rows, rows), 1)
    rank = jnp.dot(named.astype(bf16), before.astype(f32).astype(bf16), preferred_element_type=f32)
    place = lax.broadcasted_iota(jnp.int32, (128, rows), 0)
    want = jnp.zeros((groups, 128), f32)
    mine = []
    for k in range(far):
        own = jnp.sum(hits[k]*rank, axis=0, keepdims=True).astype(jnp.int32)
        rank = rank + hits[k]
        mine.append(own)
        o = owner_ref[k:k+1, :]
        dy = (lax.shift_right_logical(o, 1) - my_y) & 3
        dc = (o - my_core) & 1
        value = (dy*64 + dc*32 + slot_ref[k:k+1, :]).astype(f32)
        at = jnp.where(place == own, value, 0.0)
        want = want + lax.dot_general(hits[k].astype(bf16), at.astype(bf16), (((1,), (1,)), ((), ())),
                                      preferred_element_type=f32)
    want_ref[...] = want.astype(jnp.int32)
    base = []
    for k in range(far):
        asked = lax.shift_right_logical(owner_ref[k:k+1, :], 3)
        late = groups*PER_A + asked*PER_B + (mine[k]-FIRST)*6
        base.append(jnp.where(mine[k] >= FIRST, late, asked*PER_A + mine[k]*6))
    order = []
    for k in range(far):
        p = jnp.zeros((1, rows), jnp.int32)
        for j in range(far):
            if j != k:
                p = p + jnp.where((mine[j] < mine[k]) if j > k else (mine[j] <= mine[k]), 1, 0)
        order.append(p)
    plan_ref[...] = jnp.zeros(plan_ref.shape, jnp.int32)
    tops = []
    for p in range(far):
        b = jnp.zeros((1, rows), jnp.int32)
        m = jnp.zeros((1, rows), jnp.int32)
        for k in range(far):
            b = b + jnp.where(order[k] == p, base[k], 0)
            if p % UNIT == UNIT-1:
                m = m + jnp.where(order[k] == p, mine[k], 0)
        plan_ref[p:p+1, 0:rows] = b
        if p % UNIT == UNIT-1:
            tops.append(m)
    top = jnp.concatenate(tops + [jnp.full((1, 128 - 2*rows), CAP, jnp.int32)], 1)
    unit = lax.broadcasted_iota(jnp.int32, (1, 128), 1)
    ready = jnp.where((top < FIRST) & (unit < 2*rows), 1.0, 0.0)
    lower = lax.broadcasted_iota(jnp.int32, (128, 128), 0) < lax.broadcasted_iota(jnp.int32, (128, 128), 1)
    ahead = jnp.dot(jnp.broadcast_to(ready, (8, 128)).astype(bf16), lower.astype(f32).astype(bf16),
                    preferred_element_type=f32)[0:1]
    count = jnp.sum(ready, axis=1, keepdims=True)
    spot = jnp.where(ready > 0.0, ahead, count + unit.astype(f32) - ahead)
    spot = jnp.transpose(jnp.broadcast_to(spot, (128, 128)))
    row = lax.broadcasted_iota(jnp.int32, (128, 128), 0)
    lane = lax.broadcasted_iota(jnp.int32, (128, 128), 1).astype(f32)
    listed = jnp.sum(jnp.where((spot == lane) & (row < 2*rows), row.astype(f32), 0.0), axis=0, keepdims=True)
    plan_ref[far:far+1, :] = listed.astype(jnp.int32)
    plan_ref[far+1:far+2, :] = jnp.broadcast_to(count, (1, 128)).astype(jnp.int32)


def pack(y_ref, f_ref, out_ref):
    for t in range(y_ref.shape[1] // 128):
        out_ref[6*t:6*t+3, :] = y_ref[:, 128*t:128*t+128]
        out_ref[6*t+3:6*t+6, :] = f_ref[:, 128*t:128*t+128]


def reply_kernel(ranks, *refs):
    ask_ref, *tables = refs[:5]
    out_ref, table_ref = refs[-2:]
    leaves = tables[0].shape[0] // 6
    for i, ref in enumerate(tables):
        for k in range(leaves):
            to = 8*(leaves*i + k)
            table_ref[to:to+6, :] = ref[6*k:6*k+6, :]

    def one(p, _):
        for q, r in enumerate(ranks):
            tile = table_ref[pl.ds(pl.multiple_of(ask_ref[p, r] * 8, 8), 8), :]
            out_ref[p, 6*q:6*q+6, :] = tile[0:6]
        return 0
    lax.fori_loop(0, out_ref.shape[0], one, 0)


def per_device(points, forces, near_leaf, far_owner, far_slot):
    n, near_count = near_leaf.shape
    far_count = far_owner.shape[1]
    groups = lax.axis_size("seg")
    i32 = jnp.int32
    want, plan, own = pl.pallas_call(
        request_kernel,
        out_shape=(jax.ShapeDtypeStruct((groups, 128), i32), jax.ShapeDtypeStruct((far_count + 2, 128), i32),
                   jax.ShapeDtypeStruct((6*n, 128), f32)),
        in_specs=[VM]*4, out_specs=(VM, VM, VM), name="requests",
    )(far_owner.T, far_slot.T, points, forces)

    def send(values):
        return lax.all_to_all(values, "seg", split_axis=0, concat_axis=0, tiled=True)
    asked = send(want.reshape(groups, 1, 128)).reshape(groups, 128)

    chip = jnp.concatenate([own, lax.ppermute(own, "core", [(0, 1), (1, 0)])], 0)
    tables = [chip] + [lax.ppermute(chip, "y", [(i, (i - d) % 4) for i in range(4)]) for d in (1, 2, 3)]

    def answer(per, ranks, *after):
        reply = pl.pallas_call(
            functools.partial(reply_kernel, ranks),
            out_shape=jax.ShapeDtypeStruct((groups, per, 128), f32),
            in_specs=[SM] + [VM]*(4 + len(after)), out_specs=VM,
            scratch_shapes=[pltpu.VMEM((64*n, 128), f32)], name="replies",
            compiler_params=pltpu.CompilerParams(vmem_limit_bytes=32 << 20),
        )(asked, *tables, *after)
        return reply, send(reply).reshape(-1, 128)
    reply_a, answers_a = answer(PER_A, range(0, FIRST))
    near = pairs("near", near_count, (near_leaf.T, asked), (points, forces))
    reply_b, answers_b = answer(PER_B, range(FIRST, CAP), near)
    first = pairs("first", UNIT, (plan,), (points, near, answers_a))
    return pairs("rest", UNIT, (plan,), (points, first, answers_a, answers_b))


def solution(mesh):
    grid = jax.sharding.Mesh(mesh.devices.reshape(mesh.devices.shape[0], -1, 2), ("seg", "y", "core"))
    every = ("seg", "y", "core")
    split = P(None, every)
    rows = P(every, None)
    return jax.shard_map(
        per_device, mesh=grid, in_specs=(split, split, rows, rows, rows), out_specs=split, check_vma=False
    )
```
